256 devices in a mesh: dp: 16 (over y, x), mp: 16 (over z, core).
Axes of the slice: x: 4, y: 4, z: 8, core: 2. Of those that a mesh axis runs over, the one named last changes fastest.
Arguments:
- output_cotangent: bfloat16 [16384, 8192], P(('dp', 'mp')), may hold values from -6 to 6
- acts: bfloat16 [16384, 8192], P('dp', 'mp'), may hold values from -6 to 6
- output_weight: bfloat16 [8192, 8192], P('mp'), may hold values from -0.0625 to 0.0625
- adapter_down_weight: bfloat16 [64, 8192, 16], P('dp', 'mp'), may hold values from -0.0625 to 0.0625
- adapter_up_weight: bfloat16 [64, 16, 8192], P('dp', None, 'mp'), may hold values from -0.0625 to 0.0625
- counts: int32 [64], replicated, may hold values from 1 to 4224, as said below
- block_tenant_map: int32 [128], replicated, may hold values from 0 to 63, as said below
- owner: int32 [64], replicated, may hold values from 0 to 63, each once
Outputs:
- input_gradient: bfloat16 [16384, 8192], P('dp', 'mp')
- grad_down: float32 [64, 8192, 16], P('dp', 'mp')
- grad_up: float32 [64, 16, 8192], P('dp', None, 'mp')
The draws below stay inside these ranges and needn't reach their ends.
Inputs may be any that keep to these rules, and one draw needn't show every extreme that they name: Each tenant's blocks stand together in block_tenant_map, and every tenant has one block or more. `counts`: A tenant with n blocks has a count from 128 * (n - 1) + 1 to 128 * n.
All inputs are finite; a program needn't handle non-finite values.
Results may differ from the reference program's by a relative error of at most 0.0034.
Values may be sent and summed in bfloat16 or wider, within the bound.
No kernel may reach another device: no remote copies, remote signals or barrier semaphores. Data moves between devices by JAX's collectives and lax.ppermute only.
A program may use at most 128 MiB of HBM per device.

```python
import jax
import jax.numpy as jnp

MODEL_WIDTH = 8192
ADAPTER_RANK = 16
BLOCK = 128
INPUT_FEATURES = 8192
TOKENS = 16384
NBLK = 128
TENANT_COUNT = 64


def tenant_layout(key):
    first_key, second_key, order_key, place_key = jax.random.split(key, 4)
    spare = NBLK - TENANT_COUNT
    heavy_extra = spare - spare // 2
    rest = spare // 2
    first = jax.random.randint(first_key, (rest,), 0, TENANT_COUNT)
    second = jax.random.randint(second_key, (rest,), 0, TENANT_COUNT)
    ranked = first * second // TENANT_COUNT
    order = jax.random.permutation(order_key, TENANT_COUNT).astype(jnp.int32)
    chosen = order[1 + ranked % max(TENANT_COUNT - 2, 1)]
    tenant_ids = jnp.arange(TENANT_COUNT, dtype=jnp.int32)
    blocks = 1 + jnp.sum((chosen[:, None] == tenant_ids[None, :]).astype(jnp.int32), axis=0)
    blocks = blocks + heavy_extra * (tenant_ids == order[0]).astype(jnp.int32)
    placing = jax.random.permutation(place_key, TENANT_COUNT).astype(jnp.int32)
    ends = jnp.cumsum(blocks[placing])
    block_ids = jnp.arange(NBLK, dtype=jnp.int32)
    position = jnp.sum((ends[None, :] <= block_ids[:, None]).astype(jnp.int32), axis=1)
    block_tenant_map = placing[position].astype(jnp.int32)
    return (blocks.astype(jnp.int32), block_tenant_map, order)


def draw_counts(key, part):
    blocks, block_tenant_map, order = tenant_layout(key)
    key = jax.random.fold_in(key, 11)
    last = jax.random.randint(key, (TENANT_COUNT,), 1, BLOCK + 1).astype(jnp.int32)
    tenant_ids = jnp.arange(TENANT_COUNT, dtype=jnp.int32)
    last = jnp.where(tenant_ids == order[0], BLOCK, last)
    last = jnp.where(tenant_ids == order[TENANT_COUNT - 1], 1, last)
    return ((blocks - 1) * BLOCK + last).astype(jnp.int32)


def draw_block_tenant_map(key, part):
    blocks, block_tenant_map, order = tenant_layout(key)
    return block_tenant_map


def level_of(key, shape, shards, low, high):
    factor_of, own = 1.0, jax.random.fold_in(key, 6)
    for dim, parts in shards:
        heights = jnp.exp(jax.random.uniform(jax.random.fold_in(own, dim), (parts,), jnp.float32, low / len(shards), high / len(shards)))
        factor_of = factor_of * jnp.repeat(heights, shape[dim] // parts).reshape([-1 if axis == dim else 1 for axis in range(len(shape))])
    return factor_of


def noise(rng, extent, scale, most, cuts=(), kind=jnp.bfloat16):
    values = jax.random.normal(rng, extent, jnp.float32) * scale
    if len(cuts) > 0:
        values = level_of(rng, extent, cuts, -0.22, 0.18) * values
    return jnp.clip(values, min=-most, max=most).astype(kind)


def setup_inputs(seed: int = 0) -> dict:
    splits = jax.random.split(jax.random.key(seed), 9)
    output_cotangent = noise(splits[0], (TOKENS, MODEL_WIDTH), 1.0, 6.0, ((0, 256),))
    acts = noise(splits[1], (TOKENS, INPUT_FEATURES), 1.0, 6.0, ((0, 16), (1, 16)))
    output_weight = noise(splits[2], (INPUT_FEATURES, MODEL_WIDTH), MODEL_WIDTH ** -0.5, 0.0625, ((0, 16),))
    adapter_down_weight = noise(splits[3], (TENANT_COUNT, INPUT_FEATURES, ADAPTER_RANK), INPUT_FEATURES ** -0.5, 0.0625, ((0, 16), (1, 16)))
    adapter_up_weight = noise(splits[4], (TENANT_COUNT, ADAPTER_RANK, MODEL_WIDTH), MODEL_WIDTH ** -0.5, 0.0625, ((0, 16), (2, 16)))
    counts = draw_counts(jax.random.fold_in(splits[8], 71), 0)
    block_tenant_map = draw_block_tenant_map(jax.random.fold_in(splits[8], 71), 0)
    owner = jax.random.permutation(splits[7], TENANT_COUNT).astype(jnp.int32)
    return dict(output_cotangent=output_cotangent, acts=acts, output_weight=output_weight, adapter_down_weight=adapter_down_weight, adapter_up_weight=adapter_up_weight, counts=counts, block_tenant_map=block_tenant_map, owner=owner)


adapter_scale = 2.0


def reference(output_cotangent, acts, output_weight, adapter_down_weight, adapter_up_weight, counts, block_tenant_map, owner):
    gathered_rows = output_cotangent.shape[0]
    nblocks = block_tenant_map.shape[0]
    index = jnp.arange(nblocks, dtype=jnp.int32)
    same = (block_tenant_map[:, None] == block_tenant_map[None, :]) & (index[None, :] < index[:, None])
    before = jnp.sum(same.astype(jnp.int32), axis=1).astype(jnp.int32)
    limit = counts[block_tenant_map].astype(jnp.int32)
    within = jnp.arange(BLOCK, dtype=jnp.int32)
    valid = (before[:, None] * BLOCK + within[None, :]) < limit[:, None]
    blocks_out = output_cotangent.reshape(nblocks, BLOCK, MODEL_WIDTH)
    masked_rows = jnp.where(valid[:, :, None], blocks_out, jnp.zeros_like(blocks_out))
    adapter_slots = owner[block_tenant_map].astype(jnp.int32)
    down_factor = adapter_down_weight[adapter_slots]
    up_factor = adapter_up_weight[adapter_slots]
    activation_block = acts.reshape(nblocks, BLOCK, INPUT_FEATURES)
    reduced_product = jnp.einsum('nbh,nhr->nbr', activation_block.astype(jnp.float32), down_factor.astype(jnp.float32)).astype(jnp.bfloat16)
    backward_term = jnp.einsum('nbd,nrd->nbr', masked_rows.astype(jnp.float32), up_factor.astype(jnp.float32)).astype(jnp.bfloat16)
    frozen_term = jnp.dot(masked_rows.reshape(gathered_rows, MODEL_WIDTH), output_weight.T, preferred_element_type=jnp.float32)
    adapter_extra = jnp.einsum('nbr,nhr->nbh', backward_term.astype(jnp.float32), down_factor.astype(jnp.float32))
    input_gradient = (frozen_term + adapter_scale * adapter_extra.reshape(gathered_rows, INPUT_FEATURES)).astype(jnp.bfloat16)
    down_factor_block = adapter_scale * jnp.einsum('fay,fat->fyt', activation_block.astype(jnp.float32), backward_term.astype(jnp.float32))
    up_factor_block = adapter_scale * jnp.einsum('wqk,wqj->wkj', reduced_product.astype(jnp.float32), masked_rows.astype(jnp.float32))
    tenants = owner.shape[0]
    grad_down = jax.ops.segment_sum(down_factor_block, adapter_slots, num_segments=tenants)
    grad_up = jax.ops.segment_sum(up_factor_block, adapter_slots, num_segments=tenants)
    return input_gradient, grad_down, grad_up
```

```python
import jax
import jax.numpy as jnp
from jax import lax
from jax.experimental import pallas as pl
from jax.experimental.pallas import tpu as pltpu
from jax.sharding import PartitionSpec as P

BLOCK = 128
SIDE = 4
CORES = 2
STEP_K = 1024


adapter_scale = 2.0


def ring_step(shift, ring):
    return [
        (z * CORES + c, ((z + shift) % ring) * CORES + c)
        for z in range(ring)
        for c in range(CORES)
    ]


def x_step(shift):
    return [
        (y * SIDE + x, y * SIDE + (x + shift) % SIDE) for y in range(SIDE) for x in range(SIDE)
    ]


def y_step(shift):
    return [
        (y * SIDE + x, ((y + shift) % SIDE) * SIDE + x) for y in range(SIDE) for x in range(SIDE)
    ]


def frozen_kernel(n, place_ref, *refs):
    shards, weight = refs[:n], refs[n]
    out, total, sems = refs[-3:]
    rows = shards[0].shape[0]
    step = pl.program_id(0)
    left = jnp.concatenate([s[...] for s in shards], axis=0)
    part = lax.dot_general(
        left, weight[...], (((1,), (1,)), ((), ())), preferred_element_type=jnp.float32
    )

    @pl.when(step == 0)
    def _():
        total[...] = part

    @pl.when(step > 0)
    def _():
        total[...] += part

    @pl.when(step == pl.num_programs(0) - 1)
    def _():
        copies = [
            pltpu.make_async_copy(
                total.at[pl.ds(i * rows, rows)],
                out.at[pl.ds(pl.multiple_of(place_ref[i] * rows, rows), rows)],
                sems.at[i],
            )
            for i in range(n)
        ]
        for copy in copies:
            copy.start()
        for copy in copies:
            copy.wait()


def frozen_rows(places, shards, weight, all_rows, held=()):
    n = len(shards)
    rows, width = shards[0].shape
    features = weight.shape[0]
    grid_spec = pltpu.PrefetchScalarGridSpec(
        num_scalar_prefetch=1,
        grid=(width // STEP_K,),
        in_specs=[pl.BlockSpec((rows, STEP_K), lambda k, p: (0, k))] * n
        + [
            pl.BlockSpec((features, STEP_K), lambda k, p: (0, k)),
        ]
        + [pl.BlockSpec(memory_space=pl.ANY)] * len(held),
        out_specs=pl.BlockSpec(memory_space=pl.ANY),
        scratch_shapes=[
            pltpu.VMEM((n * rows, features), jnp.float32),
            pltpu.SemaphoreType.DMA((n,)),
        ],
    )
    return pl.pallas_call(
        lambda *refs: frozen_kernel(n, *refs),
        out_shape=jax.ShapeDtypeStruct((all_rows, features), jnp.float32),
        grid_spec=grid_spec,
        input_output_aliases={n + 2: 0} if held else {},
        compiler_params=pltpu.CompilerParams(vmem_limit_bytes=24 * 1024 * 1024),
        cost_estimate=pl.CostEstimate(
            flops=2 * n * rows * width * features,
            bytes_accessed=2 * width * (features + n * rows),
            transcendentals=0,
        ),
    )(jnp.stack(places).astype(jnp.int32), *shards, weight, *held)


def per_device(
    output_cotangent,
    acts,
    output_weight,
    adapter_down_weight,
    adapter_up_weight,
    counts,
    block_tenant_map,
    owner,
):
    f32, bf16 = jnp.float32, jnp.bfloat16
    shard_rows, width = output_cotangent.shape
    features = acts.shape[1]
    held_slots, rank, columns = adapter_up_weight.shape
    nblk_loc = acts.shape[0] // BLOCK
    mp = width // columns
    ring = mp // CORES
    slot_count = owner.shape[0]
    nblocks = block_tenant_map.shape[0]
    group = lax.axis_index("dp")
    member = lax.axis_index("mp")
    z, core = member // CORES, member % CORES
    y, x = group // SIDE, group % SIDE

    def up_ring(v):
        return lax.ppermute(v, "mp", ring_step(1, ring))

    def down_ring(v):
        return lax.ppermute(v, "mp", ring_step(-1, ring))

    def swap(v):
        return lax.ppermute(v, "mp", [(i, i ^ 1) for i in range(mp)])

    own = output_cotangent
    half = shard_rows // 2
    u1, d1 = up_ring(own), down_ring(own)
    u2, d2 = up_ring(u1), down_ring(d1)
    u3, d3 = up_ring(u2), down_ring(d2)
    u4, d4 = up_ring(u3[:half]), down_ring(d3[half:])
    s4 = jnp.concatenate([u4, d4], axis=0)

    tenant_ids = jnp.arange(slot_count, dtype=jnp.int32)
    global_ids = jnp.arange(nblocks, dtype=jnp.int32)
    slot_blk = jnp.sum(
        jnp.where(block_tenant_map[:, None] == tenant_ids[None, :], owner[None, :], 0), axis=1
    )
    first_block = group * nblk_loc
    local_map = lax.dynamic_slice_in_dim(block_tenant_map, first_block, nblk_loc)
    local_ids = first_block + jnp.arange(nblk_loc, dtype=jnp.int32)
    same = (local_map[:, None] == block_tenant_map[None, :]) & (
        global_ids[None, :] < local_ids[:, None]
    )
    before = jnp.sum(same.astype(jnp.int32), axis=1)
    hit = local_map[:, None] == tenant_ids[None, :]
    limit = jnp.sum(jnp.where(hit, counts[None, :], 0), axis=1)
    real = limit - before * BLOCK
    within = jnp.arange(BLOCK, dtype=jnp.int32)
    valid = within[None, :] < real[:, None]
    own_real = lax.dynamic_slice_in_dim(real, z, 1) - core * shard_rows
    own_valid = jnp.arange(shard_rows, dtype=jnp.int32) < own_real
    own_masked = jnp.where(own_valid[:, None], own, jnp.zeros_like(own))

    shifts = (0, 1, -1, 2)

    def x_gather(v):
        return [v] + [lax.ppermute(v, "dp", x_step(s)) for s in shifts[1:]]

    def y_exchange(vs):
        return [vs[0]] + [lax.ppermute(v, "dp", y_step(s)) for s, v in zip(shifts[1:], vs[1:])]

    x_sources = [y * SIDE + (x - s) % SIDE for s in shifts]
    y_targets = [((y + s) % SIDE) * SIDE + x for s in shifts]

    def slots_of(g):
        return g * held_slots + jnp.arange(held_slots, dtype=jnp.int32)

    def blocks_of(g):
        return lax.dynamic_slice_in_dim(slot_blk, g * nblk_loc, nblk_loc)

    mine = jnp.concatenate([jnp.swapaxes(adapter_down_weight, 1, 2), adapter_up_weight], axis=2)
    near = jnp.concatenate(x_gather(mine), axis=0)
    near_slots = jnp.concatenate([slots_of(g) for g in x_sources])
    picked = [
        jnp.einsum(
            "ns,srd->nrd",
            (blocks_of(g)[:, None] == near_slots[None, :]).astype(bf16),
            near,
            preferred_element_type=f32,
        ).astype(bf16)
        for g in y_targets
    ]
    got = y_exchange(picked)
    factors = got[0] + got[1] + got[2] + got[3]
    down_factor, up_factor = factors[:, :, :features], factors[:, :, features:]

    activation_block = acts.reshape(nblk_loc, BLOCK, features)
    low_part = jnp.einsum(
        "nbh,nrh->nrb", activation_block, down_factor, preferred_element_type=f32
    )
    low_high = lax.reduce_precision(low_part, 8, 7)
    low_rest = low_part - low_high
    to_rows = jnp.concatenate([up_factor, low_high.astype(bf16), low_rest.astype(bf16)], axis=2)
    to_rows = jnp.broadcast_to(to_rows[:, None], (ring, CORES) + to_rows.shape[1:])
    to_rows = to_rows.reshape((mp,) + to_rows.shape[2:])
    at_rows = lax.all_to_all(to_rows, "mp", 0, 0, tiled=True)
    low_sum = jnp.sum(
        at_rows[:, :, columns : columns + BLOCK].astype(f32)
        + at_rows[:, :, columns + BLOCK :].astype(f32),
        axis=0,
    ).astype(bf16)
    low_own = lax.dynamic_slice_in_dim(low_sum, core * shard_rows, shard_rows, 1)
    up_whole = jnp.swapaxes(at_rows[:, :, :columns], 0, 1).reshape(rank, width)
    back_own = lax.dot_general(
        up_whole, own_masked, (((1,), (1,)), ((), ())), preferred_element_type=f32
    ).astype(bf16)
    up_rows = (
        adapter_scale
        * lax.dot_general(
            low_own, own_masked, (((1,), (0,)), ((), ())), preferred_element_type=f32
        )
    ).astype(bf16)
    to_columns = jnp.swapaxes(up_rows.reshape(rank, mp, columns), 0, 1)
    back_pad = jnp.pad(back_own, ((0, 0), (0, BLOCK - shard_rows)))
    to_columns = jnp.concatenate(
        [to_columns, jnp.broadcast_to(back_pad[None], (mp, rank, BLOCK))], axis=2
    )
    at_columns = lax.all_to_all(to_columns, "mp", 0, 0, tiled=True)
    up_block = jnp.sum(
        at_columns[:, :, :columns].astype(f32).reshape(ring, CORES, rank, columns), axis=1
    )
    back = at_columns[:, :, columns : columns + shard_rows].reshape(ring, CORES, rank, shard_rows)
    back = jnp.swapaxes(back, 1, 2).reshape(nblk_loc, rank, BLOCK)
    down_block = adapter_scale * jnp.einsum(
        "nrb,nbh->nrh", back, activation_block, preferred_element_type=f32
    )

    grads = jnp.concatenate([down_block, up_block], axis=2).astype(bf16)
    near_grads = jnp.concatenate(x_gather(grads), axis=0)
    near_blocks = jnp.concatenate([blocks_of(g) for g in x_sources])
    summed = [
        jnp.einsum(
            "sn,nrd->srd",
            (slots_of(g)[:, None] == near_blocks[None, :]).astype(bf16),
            near_grads,
            preferred_element_type=f32,
        )
        for g in y_targets
    ]
    arrived = y_exchange([summed[0]] + [s.astype(bf16) for s in summed[1:]])
    total = arrived[0] + (
        arrived[1].astype(f32) + arrived[2].astype(f32) + arrived[3].astype(f32)
    )
    grad_down = jnp.swapaxes(total[:, :, :features], 1, 2)
    grad_up = total[:, :, features:]

    def places(*shifts):
        found = []
        for s in shifts:
            chip = (z + s) % ring
            found += [chip * CORES + core, chip * CORES + 1 - core]
        return found

    steps = [
        (places(0, -1, 1), [own, swap(own), u1, swap(u1), d1, swap(d1)]),
        (places(-2, 2), [u2, swap(u2), d2, swap(d2)]),
        (places(-3, 3), [u3, swap(u3), d3, swap(d3)]),
        (places(4), [s4, swap(s4)]),
    ]
    held = ()
    for where, shards in steps:
        held = (frozen_rows(where, shards, output_weight, nblk_loc * BLOCK, held),)
    frozen = held[0]
    adapter_extra = jnp.einsum(
        "nrb,nrh->nbh", back, down_factor, preferred_element_type=f32
    )
    input_gradient = jnp.where(
        valid[:, :, None],
        frozen.reshape(nblk_loc, BLOCK, features) + adapter_scale * adapter_extra,
        0.0,
    ).astype(bf16)
    return (input_gradient.reshape(nblk_loc * BLOCK, features), grad_down, grad_up)


def solution(mesh):
    in_specs = (
        P(("dp", "mp"), None),
        P("dp", "mp"),
        P("mp", None),
        P("dp", "mp", None),
        P("dp", None, "mp"),
        P(),
        P(),
        P(),
    )
    out_specs = (P("dp", "mp"), P("dp", "mp", None), P("dp", None, "mp"))
    return jax.shard_map(
        per_device, mesh=mesh, in_specs=in_specs, out_specs=out_specs, check_vma=False
    )
```

```python
import jax
import jax.numpy as jnp
from jax import lax
from jax.experimental import pallas as pl
from jax.experimental.pallas import tpu as pltpu
from jax.sharding import PartitionSpec as P

BLOCK = 128
SIDE = 4
CORES = 2
SHIFTS = (0, 1, -1, 2)
STEP_K = 2048
VMEM_BYTES = 56 * 1024 * 1024


adapter_scale = 2.0


def ring_step(shift, ring):
    return [
        (z * CORES + c, ((z + (shift if c == 0 else -shift)) % ring) * CORES + c)
        for z in range(ring)
        for c in range(CORES)
    ]


def x_step(shift):
    return [
        (y * SIDE + x, y * SIDE + (x + shift) % SIDE) for y in range(SIDE) for x in range(SIDE)
    ]


def y_step(shift):
    return [
        (y * SIDE + x, ((y + shift) % SIDE) * SIDE + x) for y in range(SIDE) for x in range(SIDE)
    ]


def dot(a, b, dims):
    return lax.dot_general(a, b, (dims, ((), ())), preferred_element_type=jnp.float32)


def local_call(kernel, out_shapes, scalars, arrays, flops=0):
    size = sum(a.size * a.dtype.itemsize for a in arrays)
    size += sum(o.size * o.dtype.itemsize for o in out_shapes)
    return pl.pallas_call(
        kernel,
        out_shape=tuple(out_shapes),
        in_specs=[pl.BlockSpec(memory_space=pltpu.SMEM)] * len(scalars)
        + [pl.BlockSpec(memory_space=pltpu.VMEM)] * len(arrays),
        out_specs=tuple([pl.BlockSpec(memory_space=pltpu.VMEM)] * len(out_shapes)),
        compiler_params=pltpu.CompilerParams(vmem_limit_bytes=16 * 1024 * 1024),
        cost_estimate=pl.CostEstimate(flops=flops, bytes_accessed=size, transcendentals=0),
    )(*scalars, *arrays)


def split_kernel(at_ref, real_ref, own, mine, other):
    z, core = at_ref[2], at_ref[3]
    rows, columns = own.shape[0], own.shape[1] // 16
    limit = real_ref[z] - core * rows
    keep = lax.broadcasted_iota(jnp.int32, (rows, columns), 0) < limit
    for r in range(mine.shape[1] // columns):
        a = own[:, (2 * r) * columns : (2 * r + 1) * columns]
        b = own[:, (2 * r + 1) * columns : (2 * r + 2) * columns]
        a = jnp.where(keep, a, jnp.zeros_like(a))
        b = jnp.where(keep, b, jnp.zeros_like(b))
        here = pl.ds(r * columns, columns)
        mine[:, here] = jnp.where(core == 0, a, b)
        other[:, here] = jnp.where(core == 0, b, a)


def pick_kernel(at_ref, slot_ref, *refs):
    near, picked = refs[:SIDE], refs[SIDE:]
    x, y = at_ref[0], at_ref[1]
    per, held = picked[0].shape[0], near[0].shape[0]
    for shift, out in zip(SHIFTS, picked):
        group = lax.rem(y + shift + SIDE, SIDE) * SIDE + x
        for n in range(per):
            slot = slot_ref[group * per + n]
            owner = slot // held
            away = lax.rem(x - owner % SIDE + SIDE, SIDE)
            here = slot % held
            value = jnp.zeros(out.shape[1:], out.dtype)
            for source, block in zip(SHIFTS, near):
                value = jnp.where(away == source % SIDE, block[here], value)
            out[n] = jnp.where(owner // SIDE == y, value, jnp.zeros_like(value))


def low_kernel(*refs):
    got, (acts, down, to_rows) = refs[:SIDE], refs[SIDE:]
    features = acts.shape[1]
    columns = to_rows.shape[2] - 2 * BLOCK
    for n in range(down.shape[0]):
        mixed = sum(g[n].astype(jnp.float32) for g in got).astype(jnp.bfloat16)
        factor = mixed[:, :features]
        down[n] = factor
        low = dot(factor, acts[pl.ds(n * BLOCK, BLOCK), :], ((1,), (1,)))
        high = low.astype(jnp.bfloat16)
        to_rows[n, :, :columns] = mixed[:, features:]
        to_rows[n, :, columns : columns + BLOCK] = high
        to_rows[n, :, columns + BLOCK :] = (low - high.astype(jnp.float32)).astype(jnp.bfloat16)


def sums_kernel(at_ref, at_rows, mine, other, sums):
    core = at_ref[3]
    ring, rank, size = at_rows.shape
    columns = size - 2 * BLOCK
    low = jnp.zeros((rank, BLOCK), jnp.float32)
    back_mine = jnp.zeros((rank, mine.shape[0]), jnp.float32)
    back_other = jnp.zeros((rank, mine.shape[0]), jnp.float32)
    for r in range(ring):
        low += at_rows[r, :, columns : columns + BLOCK].astype(jnp.float32)
        low += at_rows[r, :, columns + BLOCK :].astype(jnp.float32)
        up = at_rows[r, :, :columns]
        here = pl.ds(r * columns, columns)
        back_mine += dot(up, mine[:, here], ((1,), (1,)))
        back_other += dot(up, other[:, here], ((1,), (1,)))
    first = jnp.where(core == 0, back_mine, back_other)
    second = jnp.where(core == 0, back_other, back_mine)
    sums[:rank] = low
    sums[rank:] = jnp.concatenate([first, second], axis=1)


def columns_kernel(at_ref, sums, more, mine, other, to_columns):
    core = at_ref[3]
    rank, rows = sums.shape[0] // 2, mine.shape[0]
    whole = (sums[...] + more[...]).astype(jnp.bfloat16)
    low, back = whole[:rank], whole[rank:]
    first, second = low[:, :rows], low[:, rows:]
    low_mine = jnp.where(core == 0, first, second)
    low_other = jnp.where(core == 0, second, first)
    columns = to_columns.shape[2] - BLOCK
    for r in range(to_columns.shape[0]):
        here = pl.ds(r * columns, columns)
        value = dot(low_mine, mine[:, here], ((1,), (0,)))
        value += dot(low_other, other[:, here], ((1,), (0,)))
        to_columns[r, :, :columns] = (adapter_scale * value).astype(jnp.bfloat16)
        to_columns[r, :, columns:] = back


def grads_kernel(at_columns, acts, grads):
    features = acts.shape[1]
    columns = at_columns.shape[2] - BLOCK
    count = at_columns.shape[0]
    for n in range(count):
        back = at_columns[n, :, columns:]
        value = adapter_scale * dot(back, acts[pl.ds(n * BLOCK, BLOCK), :], ((1,), (0,)))
        grads[n, :, :features] = value.astype(jnp.bfloat16)
        grads[n, :, features:] = at_columns[n, :, :columns]


def slots_kernel(at_ref, slot_ref, *refs):
    near, summed, total = refs[:SIDE], refs[SIDE:-1], refs[-1]
    x, y = at_ref[0], at_ref[1]
    per, held = near[0].shape[0], summed[0].shape[0]
    total[...] = jnp.zeros_like(total)
    for shift, block in zip(SHIFTS, near):
        group = y * SIDE + lax.rem(x - shift + SIDE, SIDE)
        for n in range(per):
            slot = slot_ref[group * per + n]
            owner = slot // held

            @pl.when(owner % SIDE == x)
            def _():
                here = (owner // SIDE) * held + slot % held
                total[here] = total[here] + block[n].astype(jnp.float32)

    for shift, out in zip(SHIFTS, summed):
        there = lax.rem(y + shift + SIDE, SIDE) * held
        out[...] = total[pl.ds(there, held)].astype(jnp.bfloat16)


def finish_kernel(*refs):
    arrived, (grad_down, grad_up) = refs[:SIDE], refs[SIDE:]
    features = grad_down.shape[2]
    for s in range(grad_down.shape[0]):
        value = sum(a[s].astype(jnp.float32) for a in arrived)
        grad_down[s] = value[:, :features]
        grad_up[s] = value[:, features:]


def early_kernel(n, *refs):
    shards, (weight, total) = refs[:n], refs[n:]
    step = pl.program_id(0)
    left = jnp.concatenate([s[...] for s in shards], axis=0)
    part = dot(left, weight[...], ((1,), (1,)))

    @pl.when(step == 0)
    def _():
        total[...] = part

    @pl.when(step > 0)
    def _():
        total[...] += part


def early_rows(shards, weight):
    n = len(shards)
    rows, width = shards[0].shape
    features = weight.shape[0]
    return pl.pallas_call(
        lambda *refs: early_kernel(n, *refs),
        out_shape=jax.ShapeDtypeStruct((n * rows, features), jnp.float32),
        grid=(width // STEP_K,),
        in_specs=[pl.BlockSpec((rows, STEP_K), lambda k: (0, k))] * n
        + [pl.BlockSpec((features, STEP_K), lambda k: (0, k))],
        out_specs=pl.BlockSpec((n * rows, features), lambda k: (0, 0)),
        compiler_params=pltpu.CompilerParams(vmem_limit_bytes=VMEM_BYTES),
        cost_estimate=pl.CostEstimate(
            flops=2 * n * rows * width * features,
            bytes_accessed=2 * width * (features + n * rows),
            transcendentals=0,
        ),
    )(*shards, weight)


def frozen_kernel(n, early, place_ref, real_ref, *refs):
    shards, weight, at_columns, down = refs[:n], refs[n], refs[n + 1], refs[n + 2]
    before = refs[n + 3 : n + 3 + early]
    out, total, extra, done, sems = refs[-5:]
    rows = shards[0].shape[0]
    step = pl.program_id(0)
    left = jnp.concatenate([s[...] for s in shards], axis=0)
    part = dot(left, weight[...], ((1,), (1,)))

    @pl.when(step == 0)
    def _():
        total[...] = part

    @pl.when(step > 0)
    def _():
        total[...] += part

    @pl.when(step == pl.num_programs(0) - 1)
    def _():
        copies = []
        columns = at_columns.shape[2] - BLOCK
        blocks = [(a, k) for a in (*before, total) for k in range(a.shape[0] // BLOCK)]
        for i, (source, k) in enumerate(blocks):
            block = place_ref[i * CORES] // CORES
            back = at_columns[block][:, columns:]
            extra[...] = dot(back, down[block], ((0,), (0,)))
            for j in range(CORES):
                place = place_ref[i * CORES + j]
                core = place % CORES
                here = pl.ds(i * BLOCK + j * rows, rows)
                value = source[pl.ds(k * BLOCK + j * rows, rows), :]
                value = value + adapter_scale * extra[pl.ds(core * rows, rows), :]
                limit = real_ref[block] - core * rows
                keep = lax.broadcasted_iota(jnp.int32, value.shape, 0) < limit
                done[here, :] = jnp.where(keep, value, 0.0).astype(jnp.bfloat16)
                copy = pltpu.make_async_copy(
                    done.at[here, :],
                    out.at[pl.ds(pl.multiple_of(place * rows, rows), rows), :],
                    sems.at[i * CORES + j],
                )
                copy.start()
                copies.append(copy)
        for copy in copies:
            copy.wait()


def frozen_rows(places, real, shards, weight, at_columns, down, before, held=()):
    n, early, count = len(shards), len(before), len(places)
    rows, width = shards[0].shape
    features = weight.shape[0]
    all_rows = down.shape[0] * BLOCK
    whole = lambda a: pl.BlockSpec(a.shape, lambda k, p, q: (0,) * a.ndim)
    grid_spec = pltpu.PrefetchScalarGridSpec(
        num_scalar_prefetch=2,
        grid=(width // STEP_K,),
        in_specs=[pl.BlockSpec((rows, STEP_K), lambda k, p, q: (0, k))] * n
        + [
            pl.BlockSpec((features, STEP_K), lambda k, p, q: (0, k)),
            whole(at_columns),
            whole(down),
        ]
        + [whole(a) for a in before]
        + [pl.BlockSpec(memory_space=pl.ANY)] * len(held),
        out_specs=pl.BlockSpec(memory_space=pl.ANY),
        scratch_shapes=[
            pltpu.VMEM((n * rows, features), jnp.float32),
            pltpu.VMEM((BLOCK, features), jnp.float32),
            pltpu.VMEM((count * rows, features), jnp.bfloat16),
            pltpu.SemaphoreType.DMA((count,)),
        ],
    )
    return pl.pallas_call(
        lambda *refs: frozen_kernel(n, early, *refs),
        out_shape=jax.ShapeDtypeStruct((all_rows, features), jnp.bfloat16),
        grid_spec=grid_spec,
        input_output_aliases={n + early + 5: 0} if held else {},
        compiler_params=pltpu.CompilerParams(vmem_limit_bytes=VMEM_BYTES),
        cost_estimate=pl.CostEstimate(
            flops=2 * n * rows * width * features,
            bytes_accessed=2 * width * (features + n * rows),
            transcendentals=0,
        ),
    )(
        jnp.stack(places).astype(jnp.int32),
        real,
        *shards,
        weight,
        at_columns,
        down,
        *before,
        *held,
    )


def per_device(
    output_cotangent,
    acts,
    output_weight,
    adapter_down_weight,
    adapter_up_weight,
    counts,
    block_tenant_map,
    owner,
):
    f32, bf16 = jnp.float32, jnp.bfloat16
    shard_rows, width = output_cotangent.shape
    features = acts.shape[1]
    held_slots, rank, columns = adapter_up_weight.shape
    nblk_loc = acts.shape[0] // BLOCK
    mp = width // columns
    ring = mp // CORES
    slot_count = owner.shape[0]
    nblocks = block_tenant_map.shape[0]
    group = lax.axis_index("dp")
    member = lax.axis_index("mp")
    z, core = member // CORES, member % CORES
    y, x = group // SIDE, group % SIDE
    at = jnp.stack([x, y, z, core]).astype(jnp.int32)

    def ring_a(v):
        return lax.ppermute(v, "mp", ring_step(1, ring))

    def ring_b(v):
        return lax.ppermute(v, "mp", ring_step(-1, ring))

    def swap(v):
        return lax.ppermute(v, "mp", [(i, i ^ 1) for i in range(mp)])

    same_core = [[r * CORES + c for r in range(ring)] for c in range(CORES)]

    def x_exchange(v):
        return [v] + [lax.ppermute(v, "dp", x_step(shift)) for shift in SHIFTS[1:]]

    def y_exchange(vs):
        moved = zip(SHIFTS[1:], vs[1:])
        return [vs[0]] + [lax.ppermute(v, "dp", y_step(shift)) for shift, v in moved]

    def z_exchange(v):
        return lax.all_to_all(v, "mp", 0, 0, tiled=True, axis_index_groups=same_core)

    toward = 1 - 2 * core

    def places(*steps):
        found = []
        for s in steps:
            chip = (z - s * toward + ring) % ring
            found += [chip * CORES + core, chip * CORES + 1 - core]
        return found

    def shaped(*shape, dtype=bf16):
        return jax.ShapeDtypeStruct(shape, dtype)

    own = output_cotangent
    a1, b1 = ring_a(own), ring_b(own)

    tenant_ids = jnp.arange(slot_count, dtype=jnp.int32)
    global_ids = jnp.arange(nblocks, dtype=jnp.int32)
    slot_blk = jnp.sum(
        jnp.where(block_tenant_map[:, None] == tenant_ids[None, :], owner[None, :], 0), axis=1
    )
    first_block = group * nblk_loc
    local_map = lax.dynamic_slice_in_dim(block_tenant_map, first_block, nblk_loc)
    local_ids = first_block + jnp.arange(nblk_loc, dtype=jnp.int32)
    same = (local_map[:, None] == block_tenant_map[None, :]) & (
        global_ids[None, :] < local_ids[:, None]
    )
    before = jnp.sum(same.astype(jnp.int32), axis=1)
    hit = local_map[:, None] == tenant_ids[None, :]
    limit = jnp.sum(jnp.where(hit, counts[None, :], 0), axis=1)
    real = limit - before * BLOCK

    held = jnp.concatenate([jnp.swapaxes(adapter_down_weight, 1, 2), adapter_up_weight], axis=2)
    near = x_exchange(held)
    picked = local_call(
        pick_kernel,
        [shaped(nblk_loc, rank, features + columns)] * SIDE,
        [at, slot_blk],
        near,
    )
    got = y_exchange(picked)
    mine_cols, other_cols = local_call(
        split_kernel,
        [shaped(shard_rows, width // CORES)] * CORES,
        [at, real],
        [own],
    )
    other_cols = swap(other_cols)
    a2, b2 = ring_a(a1), ring_b(b1)
    got, mine_cols, other_cols, a1, b1 = lax.optimization_barrier(
        (got, mine_cols, other_cols, a1, b1)
    )
    down_factor, to_rows = local_call(
        low_kernel,
        [shaped(nblk_loc, rank, features), shaped(nblk_loc, rank, columns + 2 * BLOCK)],
        [],
        [*got, acts],
    )
    at_rows = z_exchange(to_rows)
    early = [early_rows([own, swap(own), a1, swap(b1), b1, swap(a1)], output_weight)]
    a3, b3 = ring_a(a2), ring_b(b2)
    at_rows, early, a2, b2 = lax.optimization_barrier((at_rows, early, a2, b2))
    (sums,) = local_call(
        sums_kernel,
        [shaped(2 * rank, BLOCK, dtype=f32)],
        [at],
        [at_rows, mine_cols, other_cols],
    )
    (to_columns,) = local_call(
        columns_kernel,
        [shaped(ring, rank, columns + BLOCK)],
        [at],
        [sums, swap(sums), mine_cols, other_cols],
    )
    at_columns = z_exchange(to_columns)
    early = early + [early_rows([a2, swap(b2), b2, swap(a2)], output_weight)]
    a4 = ring_a(a3)
    at_columns, early, a3, b3 = lax.optimization_barrier((at_columns, early, a3, b3))
    (grads,) = local_call(
        grads_kernel,
        [shaped(nblk_loc, rank, features + columns)],
        [],
        [at_columns, acts],
    )
    near_grads = x_exchange(grads)
    out = frozen_rows(
        places(0, 1, -1, 2, -2, 3, -3),
        real,
        [a3, swap(b3), b3, swap(a3)],
        output_weight,
        at_columns,
        down_factor,
        early,
    )
    near_grads, out, a4 = lax.optimization_barrier((near_grads, out, a4))
    (*summed, _) = local_call(
        slots_kernel,
        [shaped(held_slots, rank, features + columns)] * SIDE
        + [shaped(SIDE * held_slots, rank, features + columns, dtype=f32)],
        [at, slot_blk],
        near_grads,
    )
    arrived = y_exchange(summed)
    input_gradient = frozen_rows(
        places(4), real, [a4, swap(a4)], output_weight, at_columns, down_factor, (), (out,)
    )
    arrived, input_gradient = lax.optimization_barrier((arrived, input_gradient))
    grad_down, grad_up = local_call(
        finish_kernel,
        [shaped(held_slots, rank, features, dtype=f32), shaped(held_slots, rank, columns, dtype=f32)],
        [],
        arrived,
    )
    return (input_gradient, jnp.swapaxes(grad_down, 1, 2), grad_up)


def solution(mesh):
    in_specs = (
        P(("dp", "mp"), None),
        P("dp", "mp"),
        P("mp", None),
        P("dp", "mp", None),
        P("dp", None, "mp"),
        P(),
        P(),
        P(),
    )
    out_specs = (P("dp", "mp"), P("dp", "mp", None), P("dp", None, "mp"))
    return jax.shard_map(
        per_device, mesh=mesh, in_specs=in_specs, out_specs=out_specs, check_vma=False
    )
```

```python
import jax
import jax.numpy as jnp
from jax import lax
from jax.experimental import pallas as pl
from jax.experimental.pallas import tpu as pltpu
from jax.sharding import PartitionSpec as P

BLOCK = 128
SIDE = 4
CORES = 2
SHIFTS = (0, 1, -1, 2)
STEP_K = 2048
VMEM_BYTES = 56 * 1024 * 1024


adapter_scale = 2.0


def ring_step(shift, ring):
    return [
        (z * CORES + c, ((z + (shift if c == 0 else -shift)) % ring) * CORES + c)
        for z in range(ring)
        for c in range(CORES)
    ]


def x_step(shift):
    return [
        (y * SIDE + x, y * SIDE + (x + shift) % SIDE) for y in range(SIDE) for x in range(SIDE)
    ]


def y_step(shift):
    return [
        (y * SIDE + x, ((y + shift) % SIDE) * SIDE + x) for y in range(SIDE) for x in range(SIDE)
    ]


def dot(a, b, dims):
    return lax.dot_general(a, b, (dims, ((), ())), preferred_element_type=jnp.float32)


def local_call(kernel, out_shapes, scalars, arrays, flops=0):
    size = sum(a.size * a.dtype.itemsize for a in arrays)
    size += sum(o.size * o.dtype.itemsize for o in out_shapes)
    return pl.pallas_call(
        kernel,
        out_shape=tuple(out_shapes),
        in_specs=[pl.BlockSpec(memory_space=pltpu.SMEM)] * len(scalars)
        + [pl.BlockSpec(memory_space=pltpu.VMEM)] * len(arrays),
        out_specs=tuple([pl.BlockSpec(memory_space=pltpu.VMEM)] * len(out_shapes)),
        compiler_params=pltpu.CompilerParams(vmem_limit_bytes=16 * 1024 * 1024),
        cost_estimate=pl.CostEstimate(flops=flops, bytes_accessed=size, transcendentals=0),
    )(*scalars, *arrays)


def split_kernel(at_ref, real_ref, own, mine, other):
    z, core = at_ref[2], at_ref[3]
    rows, columns = own.shape[0], own.shape[1] // 16
    limit = real_ref[z] - core * rows
    keep = lax.broadcasted_iota(jnp.int32, (rows, columns), 0) < limit
    for r in range(mine.shape[1] // columns):
        a = own[:, (2 * r) * columns : (2 * r + 1) * columns]
        b = own[:, (2 * r + 1) * columns : (2 * r + 2) * columns]
        a = jnp.where(keep, a, jnp.zeros_like(a))
        b = jnp.where(keep, b, jnp.zeros_like(b))
        here = pl.ds(r * columns, columns)
        mine[:, here] = jnp.where(core == 0, a, b)
        other[:, here] = jnp.where(core == 0, b, a)


def pick_kernel(at_ref, slot_ref, *refs):
    near, picked = refs[:SIDE], refs[SIDE:]
    x, y = at_ref[0], at_ref[1]
    per, held = picked[0].shape[0], near[0].shape[0]
    for shift, out in zip(SHIFTS, picked):
        group = lax.rem(y + shift + SIDE, SIDE) * SIDE + x
        for n in range(per):
            slot = slot_ref[group * per + n]
            owner = slot // held
            away = lax.rem(x - owner % SIDE + SIDE, SIDE)
            here = slot % held
            value = jnp.zeros(out.shape[1:], out.dtype)
            for source, block in zip(SHIFTS, near):
                value = jnp.where(away == source % SIDE, block[here], value)
            out[n] = jnp.where(owner // SIDE == y, value, jnp.zeros_like(value))


def low_kernel(*refs):
    got, (acts, down, to_rows) = refs[:SIDE], refs[SIDE:]
    features = acts.shape[1]
    columns = to_rows.shape[2] - 2 * BLOCK
    for n in range(down.shape[0]):
        mixed = sum(g[n].astype(jnp.float32) for g in got).astype(jnp.bfloat16)
        factor = mixed[:, :features]
        down[n] = factor
        low = dot(factor, acts[pl.ds(n * BLOCK, BLOCK), :], ((1,), (1,)))
        high = low.astype(jnp.bfloat16)
        to_rows[n, :, :columns] = mixed[:, features:]
        to_rows[n, :, columns : columns + BLOCK] = high
        to_rows[n, :, columns + BLOCK :] = (low - high.astype(jnp.float32)).astype(jnp.bfloat16)


def sums_kernel(at_ref, at_rows, mine, other, sums):
    core = at_ref[3]
    ring, rank, size = at_rows.shape
    columns = size - 2 * BLOCK
    low = jnp.zeros((rank, BLOCK), jnp.float32)
    back_mine = jnp.zeros((rank, mine.shape[0]), jnp.float32)
    back_other = jnp.zeros((rank, mine.shape[0]), jnp.float32)
    for r in range(ring):
        low += at_rows[r, :, columns : columns + BLOCK].astype(jnp.float32)
        low += at_rows[r, :, columns + BLOCK :].astype(jnp.float32)
        up = at_rows[r, :, :columns]
        here = pl.ds(r * columns, columns)
        back_mine += dot(up, mine[:, here], ((1,), (1,)))
        back_other += dot(up, other[:, here], ((1,), (1,)))
    first = jnp.where(core == 0, back_mine, back_other)
    second = jnp.where(core == 0, back_other, back_mine)
    sums[:rank] = low
    sums[rank:] = jnp.concatenate([first, second], axis=1)


def columns_kernel(at_ref, sums, more, mine, other, to_columns):
    core = at_ref[3]
    rank, rows = sums.shape[0] // 2, mine.shape[0]
    whole = (sums[...] + more[...]).astype(jnp.bfloat16)
    low, back = whole[:rank], whole[rank:]
    first, second = low[:, :rows], low[:, rows:]
    low_mine = jnp.where(core == 0, first, second)
    low_other = jnp.where(core == 0, second, first)
    columns = to_columns.shape[2] - BLOCK
    for r in range(to_columns.shape[0]):
        here = pl.ds(r * columns, columns)
        value = dot(low_mine, mine[:, here], ((1,), (0,)))
        value += dot(low_other, other[:, here], ((1,), (0,)))
        to_columns[r, :, :columns] = (adapter_scale * value).astype(jnp.bfloat16)
        to_columns[r, :, columns:] = back


def grads_kernel(at_columns, acts, grads):
    features = acts.shape[1]
    columns = at_columns.shape[2] - BLOCK
    count = at_columns.shape[0]
    for n in range(count):
        back = at_columns[n, :, columns:]
        value = adapter_scale * dot(back, acts[pl.ds(n * BLOCK, BLOCK), :], ((1,), (0,)))
        grads[n, :, :features] = value.astype(jnp.bfloat16)
        grads[n, :, features:] = at_columns[n, :, :columns]


def slots_kernel(at_ref, slot_ref, *refs):
    near, summed, total = refs[:SIDE], refs[SIDE:-1], refs[-1]
    x, y = at_ref[0], at_ref[1]
    per, held = near[0].shape[0], summed[0].shape[0]
    total[...] = jnp.zeros_like(total)
    for shift, block in zip(SHIFTS, near):
        group = y * SIDE + lax.rem(x - shift + SIDE, SIDE)
        for n in range(per):
            slot = slot_ref[group * per + n]
            owner = slot // held

            @pl.when(owner % SIDE == x)
            def _():
                here = (owner // SIDE) * held + slot % held
                total[here] = total[here] + block[n].astype(jnp.float32)

    for shift, out in zip(SHIFTS, summed):
        there = lax.rem(y + shift + SIDE, SIDE) * held
        out[...] = total[pl.ds(there, held)].astype(jnp.bfloat16)


def finish_kernel(*refs):
    arrived, (grad_down, grad_up) = refs[:SIDE], refs[SIDE:]
    features = grad_down.shape[2]
    for s in range(grad_down.shape[0]):
        value = sum(a[s].astype(jnp.float32) for a in arrived)
        grad_down[s] = value[:, :features]
        grad_up[s] = value[:, features:]


def early_kernel(n, *refs):
    shards, (weight, total) = refs[:n], refs[n:]
    step = pl.program_id(0)
    left = jnp.concatenate([s[...] for s in shards], axis=0)
    part = dot(left, weight[...], ((1,), (1,)))

    @pl.when(step == 0)
    def _():
        total[...] = part

    @pl.when(step > 0)
    def _():
        total[...] += part


def early_rows(shards, weight):
    n = len(shards)
    rows, width = shards[0].shape
    features = weight.shape[0]
    return pl.pallas_call(
        lambda *refs: early_kernel(n, *refs),
        out_shape=jax.ShapeDtypeStruct((n * rows, features), jnp.float32),
        grid=(width // STEP_K,),
        in_specs=[pl.BlockSpec((rows, STEP_K), lambda k: (0, k))] * n
        + [pl.BlockSpec((features, STEP_K), lambda k: (0, k))],
        out_specs=pl.BlockSpec((n * rows, features), lambda k: (0, 0)),
        compiler_params=pltpu.CompilerParams(vmem_limit_bytes=VMEM_BYTES),
        cost_estimate=pl.CostEstimate(
            flops=2 * n * rows * width * features,
            bytes_accessed=2 * width * (features + n * rows),
            transcendentals=0,
        ),
    )(*shards, weight)


def frozen_kernel(n, early, place_ref, real_ref, *refs):
    shards, weight, at_columns, down = refs[:n], refs[n], refs[n + 1], refs[n + 2]
    before = refs[n + 3 : n + 3 + early]
    out, total, extra, done, sems = refs[-5:]
    rows = shards[0].shape[0]
    step = pl.program_id(0)
    left = jnp.concatenate([s[...] for s in shards], axis=0)
    part = dot(left, weight[...], ((1,), (1,)))

    @pl.when(step == 0)
    def _():
        total[...] = part

    @pl.when(step > 0)
    def _():
        total[...] += part

    @pl.when(step == pl.num_programs(0) - 1)
    def _():
        copies = []
        columns = at_columns.shape[2] - BLOCK
        blocks = [(a, k) for a in (*before, total) for k in range(a.shape[0] // BLOCK)]
        for i, (source, k) in enumerate(blocks):
            block = place_ref[i * CORES] // CORES
            back = at_columns[block][:, columns:]
            extra[...] = dot(back, down[block], ((0,), (0,)))
            for j in range(CORES):
                place = place_ref[i * CORES + j]
                core = place % CORES
                here = pl.ds(i * BLOCK + j * rows, rows)
                value = source[pl.ds(k * BLOCK + j * rows, rows), :]
                value = value + adapter_scale * extra[pl.ds(core * rows, rows), :]
                limit = real_ref[block] - core * rows
                keep = lax.broadcasted_iota(jnp.int32, value.shape, 0) < limit
                done[here, :] = jnp.where(keep, value, 0.0).astype(jnp.bfloat16)
                copy = pltpu.make_async_copy(
                    done.at[here, :],
                    out.at[pl.ds(pl.multiple_of(place * rows, rows), rows), :],
                    sems.at[i * CORES + j],
                )
                copy.start()
                copies.append(copy)
        for copy in copies:
            copy.wait()


def frozen_rows(places, real, shards, weight, at_columns, down, before, held=()):
    n, early, count = len(shards), len(before), len(places)
    rows, width = shards[0].shape
    features = weight.shape[0]
    all_rows = down.shape[0] * BLOCK
    whole = lambda a: pl.BlockSpec(a.shape, lambda k, p, q: (0,) * a.ndim)
    grid_spec = pltpu.PrefetchScalarGridSpec(
        num_scalar_prefetch=2,
        grid=(width // STEP_K,),
        in_specs=[pl.BlockSpec((rows, STEP_K), lambda k, p, q: (0, k))] * n
        + [
            pl.BlockSpec((features, STEP_K), lambda k, p, q: (0, k)),
            whole(at_columns),
            whole(down),
        ]
        + [whole(a) for a in before]
        + [pl.BlockSpec(memory_space=pl.ANY)] * len(held),
        out_specs=pl.BlockSpec(memory_space=pl.ANY),
        scratch_shapes=[
            pltpu.VMEM((n * rows, features), jnp.float32),
            pltpu.VMEM((BLOCK, features), jnp.float32),
            pltpu.VMEM((count * rows, features), jnp.bfloat16),
            pltpu.SemaphoreType.DMA((count,)),
        ],
    )
    return pl.pallas_call(
        lambda *refs: frozen_kernel(n, early, *refs),
        out_shape=jax.ShapeDtypeStruct((all_rows, features), jnp.bfloat16),
        grid_spec=grid_spec,
        input_output_aliases={n + early + 5: 0} if held else {},
        compiler_params=pltpu.CompilerParams(vmem_limit_bytes=VMEM_BYTES),
        cost_estimate=pl.CostEstimate(
            flops=2 * n * rows * width * features,
            bytes_accessed=2 * width * (features + n * rows),
            transcendentals=0,
        ),
    )(
        jnp.stack(places).astype(jnp.int32),
        real,
        *shards,
        weight,
        at_columns,
        down,
        *before,
        *held,
    )


def per_device(
    output_cotangent,
    acts,
    output_weight,
    adapter_down_weight,
    adapter_up_weight,
    counts,
    block_tenant_map,
    owner,
):
    f32, bf16 = jnp.float32, jnp.bfloat16
    shard_rows, width = output_cotangent.shape
    features = acts.shape[1]
    held_slots, rank, columns = adapter_up_weight.shape
    nblk_loc = acts.shape[0] // BLOCK
    mp = width // columns
    ring = mp // CORES
    slot_count = owner.shape[0]
    nblocks = block_tenant_map.shape[0]
    group = lax.axis_index("dp")
    member = lax.axis_index("mp")
    z, core = member // CORES, member % CORES
    y, x = group // SIDE, group % SIDE
    at = jnp.stack([x, y, z, core]).astype(jnp.int32)

    def ring_a(v):
        return lax.ppermute(v, "mp", ring_step(1, ring))

    def ring_b(v):
        return lax.ppermute(v, "mp", ring_step(-1, ring))

    def swap(v):
        return lax.ppermute(v, "mp", [(i, i ^ 1) for i in range(mp)])

    same_core = [[r * CORES + c for r in range(ring)] for c in range(CORES)]

    def x_exchange(v):
        return [v] + [lax.ppermute(v, "dp", x_step(shift)) for shift in SHIFTS[1:]]

    def y_exchange(vs):
        moved = zip(SHIFTS[1:], vs[1:])
        return [vs[0]] + [lax.ppermute(v, "dp", y_step(shift)) for shift, v in moved]

    def z_exchange(v):
        return lax.all_to_all(v, "mp", 0, 0, tiled=True, axis_index_groups=same_core)

    toward = 1 - 2 * core

    def places(*steps):
        found = []
        for s in steps:
            chip = (z - s * toward + ring) % ring
            found += [chip * CORES + core, chip * CORES + 1 - core]
        return found

    def shaped(*shape, dtype=bf16):
        return jax.ShapeDtypeStruct(shape, dtype)

    own = output_cotangent
    a1, b1 = ring_a(own), ring_b(own)

    tenant_ids = jnp.arange(slot_count, dtype=jnp.int32)
    global_ids = jnp.arange(nblocks, dtype=jnp.int32)
    slot_blk = jnp.sum(
        jnp.where(block_tenant_map[:, None] == tenant_ids[None, :], owner[None, :], 0), axis=1
    )
    first_block = group * nblk_loc
    local_map = lax.dynamic_slice_in_dim(block_tenant_map, first_block, nblk_loc)
    local_ids = first_block + jnp.arange(nblk_loc, dtype=jnp.int32)
    same = (local_map[:, None] == block_tenant_map[None, :]) & (
        global_ids[None, :] < local_ids[:, None]
    )
    before = jnp.sum(same.astype(jnp.int32), axis=1)
    hit = local_map[:, None] == tenant_ids[None, :]
    limit = jnp.sum(jnp.where(hit, counts[None, :], 0), axis=1)
    real = limit - before * BLOCK

    held = jnp.concatenate([jnp.swapaxes(adapter_down_weight, 1, 2), adapter_up_weight], axis=2)
    near = x_exchange(held)
    picked = local_call(
        pick_kernel,
        [shaped(nblk_loc, rank, features + columns)] * SIDE,
        [at, slot_blk],
        near,
    )
    got = y_exchange(picked)
    mine_cols, other_cols = local_call(
        split_kernel,
        [shaped(shard_rows, width // CORES)] * CORES,
        [at, real],
        [own],
    )
    other_cols = swap(other_cols)
    a2, b2 = ring_a(a1), ring_b(b1)
    down_factor, to_rows = local_call(
        low_kernel,
        [shaped(nblk_loc, rank, features), shaped(nblk_loc, rank, columns + 2 * BLOCK)],
        [],
        [*got, acts],
    )
    at_rows = z_exchange(to_rows)
    early = [early_rows([own, swap(own), a1, swap(b1), b1, swap(a1)], output_weight)]
    a3, b3 = ring_a(a2), ring_b(b2)
    at_rows, early, a2, b2, mine_cols, other_cols = lax.optimization_barrier(
        (at_rows, early, a2, b2, mine_cols, other_cols)
    )
    (sums,) = local_call(
        sums_kernel,
        [shaped(2 * rank, BLOCK, dtype=f32)],
        [at],
        [at_rows, mine_cols, other_cols],
    )
    (to_columns,) = local_call(
        columns_kernel,
        [shaped(ring, rank, columns + BLOCK)],
        [at],
        [sums, swap(sums), mine_cols, other_cols],
    )
    at_columns = z_exchange(to_columns)
    early = early + [early_rows([a2, swap(b2), b2, swap(a2)], output_weight)]
    a4 = ring_a(a3)
    at_columns, early, a3, b3 = lax.optimization_barrier((at_columns, early, a3, b3))
    (grads,) = local_call(
        grads_kernel,
        [shaped(nblk_loc, rank, features + columns)],
        [],
        [at_columns, acts],
    )
    near_grads = x_exchange(grads)
    out = frozen_rows(
        places(0, 1, -1, 2, -2, 3, -3),
        real,
        [a3, swap(b3), b3, swap(a3)],
        output_weight,
        at_columns,
        down_factor,
        early,
    )
    near_grads, out, a4 = lax.optimization_barrier((near_grads, out, a4))
    (*summed, _) = local_call(
        slots_kernel,
        [shaped(held_slots, rank, features + columns)] * SIDE
        + [shaped(SIDE * held_slots, rank, features + columns, dtype=f32)],
        [at, slot_blk],
        near_grads,
    )
    arrived = y_exchange(summed)
    input_gradient = frozen_rows(
        places(4), real, [a4, swap(a4)], output_weight, at_columns, down_factor, (), (out,)
    )
    arrived, input_gradient = lax.optimization_barrier((arrived, input_gradient))
    grad_down, grad_up = local_call(
        finish_kernel,
        [shaped(held_slots, rank, features, dtype=f32), shaped(held_slots, rank, columns, dtype=f32)],
        [],
        arrived,
    )
    return (input_gradient, jnp.swapaxes(grad_down, 1, 2), grad_up)


def solution(mesh):
    in_specs = (
        P(("dp", "mp"), None),
        P("dp", "mp"),
        P("mp", None),
        P("dp", "mp", None),
        P("dp", None, "mp"),
        P(),
        P(),
        P(),
    )
    out_specs = (P("dp", "mp"), P("dp", "mp", None), P("dp", None, "mp"))
    return jax.shard_map(
        per_device, mesh=mesh, in_specs=in_specs, out_specs=out_specs, check_vma=False
    )
```

```python
import jax
import jax.numpy as jnp
from jax import lax
from jax.experimental import pallas as pl
from jax.experimental.pallas import tpu as pltpu
from jax.sharding import PartitionSpec as P

BLOCK = 128
SIDE = 4
CORES = 2
SHIFTS = (0, 1, -1, 2)
STEP_K = 2048
VMEM_BYTES = 56 * 1024 * 1024


adapter_scale = 2.0


def ring_step(shift, ring):
    return [
        (z * CORES + c, ((z + (shift if c == 0 else -shift)) % ring) * CORES + c)
        for z in range(ring)
        for c in range(CORES)
    ]


def x_step(shift):
    return [
        (y * SIDE + x, y * SIDE + (x + shift) % SIDE) for y in range(SIDE) for x in range(SIDE)
    ]


def y_step(shift):
    return [
        (y * SIDE + x, ((y + shift) % SIDE) * SIDE + x) for y in range(SIDE) for x in range(SIDE)
    ]


def dot(a, b, dims):
    return lax.dot_general(a, b, (dims, ((), ())), preferred_element_type=jnp.float32)


def local_call(kernel, out_shapes, scalars, arrays, flops=0, scratch=()):
    size = sum(a.size * a.dtype.itemsize for a in arrays)
    size += sum(o.size * o.dtype.itemsize for o in out_shapes)
    return pl.pallas_call(
        kernel,
        out_shape=tuple(out_shapes),
        in_specs=[pl.BlockSpec(memory_space=pltpu.SMEM)] * len(scalars)
        + [pl.BlockSpec(memory_space=pltpu.VMEM)] * len(arrays),
        out_specs=tuple([pl.BlockSpec(memory_space=pltpu.VMEM)] * len(out_shapes)),
        scratch_shapes=list(scratch),
        compiler_params=pltpu.CompilerParams(vmem_limit_bytes=16 * 1024 * 1024),
        cost_estimate=pl.CostEstimate(flops=flops, bytes_accessed=size, transcendentals=0),
    )(*scalars, *arrays)


def split_kernel(at_ref, real_ref, own, mine, other):
    z, core = at_ref[2], at_ref[3]
    rows, columns = own.shape[0], own.shape[1] // 16
    limit = real_ref[z] - core * rows
    keep = lax.broadcasted_iota(jnp.int32, (rows, columns), 0) < limit
    for r in range(mine.shape[1] // columns):
        a = own[:, (2 * r) * columns : (2 * r + 1) * columns]
        b = own[:, (2 * r + 1) * columns : (2 * r + 2) * columns]
        a = jnp.where(keep, a, jnp.zeros_like(a))
        b = jnp.where(keep, b, jnp.zeros_like(b))
        here = pl.ds(r * columns, columns)
        mine[:, here] = jnp.where(core == 0, a, b)
        other[:, here] = jnp.where(core == 0, b, a)


def pick_kernel(at_ref, slot_ref, *refs):
    near, picked = refs[:SIDE], refs[SIDE:]
    x, y = at_ref[0], at_ref[1]
    per, held = picked[0].shape[0], near[0].shape[0]
    for shift, out in zip(SHIFTS, picked):
        group = lax.rem(y + shift + SIDE, SIDE) * SIDE + x
        for n in range(per):
            slot = slot_ref[group * per + n]
            owner = slot // held
            away = lax.rem(x - owner % SIDE + SIDE, SIDE)
            here = slot % held
            value = jnp.zeros(out.shape[1:], out.dtype)
            for source, block in zip(SHIFTS, near):
                value = jnp.where(away == source % SIDE, block[here], value)
            out[n] = jnp.where(owner // SIDE == y, value, jnp.zeros_like(value))


def low_kernel(*refs):
    got, (acts, down, to_rows) = refs[:SIDE], refs[SIDE:]
    features = acts.shape[1]
    columns = to_rows.shape[2] - 2 * BLOCK
    for n in range(down.shape[0]):
        mixed = sum(g[n].astype(jnp.float32) for g in got).astype(jnp.bfloat16)
        factor = mixed[:, :features]
        down[n] = factor
        low = dot(factor, acts[pl.ds(n * BLOCK, BLOCK), :], ((1,), (1,)))
        high = low.astype(jnp.bfloat16)
        to_rows[n, :, :columns] = mixed[:, features:]
        to_rows[n, :, columns : columns + BLOCK] = high
        to_rows[n, :, columns + BLOCK :] = (low - high.astype(jnp.float32)).astype(jnp.bfloat16)


def sums_kernel(at_ref, at_rows, mine, other, sums):
    core = at_ref[3]
    ring, rank, size = at_rows.shape
    columns = size - 2 * BLOCK
    low = jnp.zeros((rank, BLOCK), jnp.float32)
    back_mine = jnp.zeros((rank, mine.shape[0]), jnp.float32)
    back_other = jnp.zeros((rank, mine.shape[0]), jnp.float32)
    for r in range(ring):
        low += at_rows[r, :, columns : columns + BLOCK].astype(jnp.float32)
        low += at_rows[r, :, columns + BLOCK :].astype(jnp.float32)
        up = at_rows[r, :, :columns]
        here = pl.ds(r * columns, columns)
        back_mine += dot(up, mine[:, here], ((1,), (1,)))
        back_other += dot(up, other[:, here], ((1,), (1,)))
    first = jnp.where(core == 0, back_mine, back_other)
    second = jnp.where(core == 0, back_other, back_mine)
    sums[:rank] = low
    sums[rank:] = jnp.concatenate([first, second], axis=1)


def columns_kernel(at_ref, sums, more, mine, other, to_columns):
    core = at_ref[3]
    rank, rows = sums.shape[0] // 2, mine.shape[0]
    whole = (sums[...] + more[...]).astype(jnp.bfloat16)
    low, back = whole[:rank], whole[rank:]
    first, second = low[:, :rows], low[:, rows:]
    low_mine = jnp.where(core == 0, first, second)
    low_other = jnp.where(core == 0, second, first)
    columns = to_columns.shape[2] - BLOCK
    for r in range(to_columns.shape[0]):
        here = pl.ds(r * columns, columns)
        value = dot(low_mine, mine[:, here], ((1,), (0,)))
        value += dot(low_other, other[:, here], ((1,), (0,)))
        to_columns[r, :, :columns] = (adapter_scale * value).astype(jnp.bfloat16)
        to_columns[r, :, columns:] = back


def grads_kernel(at_columns, acts, grads):
    features = acts.shape[1]
    columns = at_columns.shape[2] - BLOCK
    count = at_columns.shape[0]
    for n in range(count):
        back = at_columns[n, :, columns:]
        value = adapter_scale * dot(back, acts[pl.ds(n * BLOCK, BLOCK), :], ((1,), (0,)))
        grads[n, :, :features] = value.astype(jnp.bfloat16)
        grads[n, :, features:] = at_columns[n, :, :columns]


def slots_kernel(at_ref, slot_ref, *refs):
    near, summed, total = refs[:SIDE], refs[SIDE:-1], refs[-1]
    x, y = at_ref[0], at_ref[1]
    per, held = near[0].shape[0], summed[0].shape[0]
    total[...] = jnp.zeros_like(total)
    for shift, block in zip(SHIFTS, near):
        group = y * SIDE + lax.rem(x - shift + SIDE, SIDE)
        for n in range(per):
            slot = slot_ref[group * per + n]
            owner = slot // held

            @pl.when(owner % SIDE == x)
            def _():
                here = (owner // SIDE) * held + slot % held
                total[here] = total[here] + block[n].astype(jnp.float32)

    for shift, out in zip(SHIFTS, summed):
        there = lax.rem(y + shift + SIDE, SIDE) * held
        out[...] = total[pl.ds(there, held)].astype(jnp.bfloat16)


def finish_kernel(*refs):
    arrived, (grad_down, grad_up) = refs[:SIDE], refs[SIDE:]
    features = grad_down.shape[2]
    for s in range(grad_down.shape[0]):
        value = sum(a[s].astype(jnp.float32) for a in arrived)
        grad_down[s] = value[:, :features]
        grad_up[s] = value[:, features:]


def early_kernel(n, *refs):
    shards, (weight, total) = refs[:n], refs[n:]
    step = pl.program_id(0)
    left = jnp.concatenate([s[...] for s in shards], axis=0)
    part = dot(left, weight[...], ((1,), (1,)))

    @pl.when(step == 0)
    def _():
        total[...] = part

    @pl.when(step > 0)
    def _():
        total[...] += part


def early_rows(shards, weight):
    n = len(shards)
    rows, width = shards[0].shape
    features = weight.shape[0]
    return pl.pallas_call(
        lambda *refs: early_kernel(n, *refs),
        out_shape=jax.ShapeDtypeStruct((n * rows, features), jnp.float32),
        grid=(width // STEP_K,),
        in_specs=[pl.BlockSpec((rows, STEP_K), lambda k: (0, k))] * n
        + [pl.BlockSpec((features, STEP_K), lambda k: (0, k))],
        out_specs=pl.BlockSpec((n * rows, features), lambda k: (0, 0)),
        compiler_params=pltpu.CompilerParams(vmem_limit_bytes=VMEM_BYTES),
        cost_estimate=pl.CostEstimate(
            flops=2 * n * rows * width * features,
            bytes_accessed=2 * width * (features + n * rows),
            transcendentals=0,
        ),
    )(*shards, weight)


def frozen_kernel(n, early, first, place_ref, real_ref, *refs):
    shards, weight, at_columns, down = refs[:n], refs[n], refs[n + 1], refs[n + 2]
    before = refs[n + 3 : n + 3 + early]
    out, total, extra, done, sems = refs[-5:]
    rows = shards[0].shape[0]
    step = pl.program_id(0)
    left = jnp.concatenate([s[...] for s in shards], axis=0)
    part = dot(left, weight[...], ((1,), (1,)))

    @pl.when(step == 0)
    def _():
        total[...] = part

    @pl.when(step > 0)
    def _():
        total[...] += part

    @pl.when(step == pl.num_programs(0) - 1)
    def _():
        copies = []
        columns = at_columns.shape[2] - BLOCK
        blocks = [(a, k) for a in (*before, total) for k in range(a.shape[0] // BLOCK)]
        for i, (source, k) in enumerate(blocks):
            block = place_ref[first + i * CORES] // CORES
            back = at_columns[block][:, columns:]
            extra[...] = dot(back, down[block], ((0,), (0,)))
            for j in range(CORES):
                place = place_ref[first + i * CORES + j]
                core = place % CORES
                here = pl.ds(i * BLOCK + j * rows, rows)
                value = source[pl.ds(k * BLOCK + j * rows, rows), :]
                value = value + adapter_scale * extra[pl.ds(core * rows, rows), :]
                limit = real_ref[block] - core * rows
                keep = lax.broadcasted_iota(jnp.int32, value.shape, 0) < limit
                done[here, :] = jnp.where(keep, value, 0.0).astype(jnp.bfloat16)
                copy = pltpu.make_async_copy(
                    done.at[here, :],
                    out.at[pl.ds(pl.multiple_of(place * rows, rows), rows), :],
                    sems.at[i * CORES + j],
                )
                copy.start()
                copies.append(copy)
        for copy in copies:
            copy.wait()


def frozen_rows(places, first, count, real, shards, weight, at_columns, down, before, held=()):
    n, early = len(shards), len(before)
    rows, width = shards[0].shape
    features = weight.shape[0]
    all_rows = down.shape[0] * BLOCK
    whole = lambda a: pl.BlockSpec(a.shape, lambda k, p, q: (0,) * a.ndim)
    grid_spec = pltpu.PrefetchScalarGridSpec(
        num_scalar_prefetch=2,
        grid=(width // STEP_K,),
        in_specs=[pl.BlockSpec((rows, STEP_K), lambda k, p, q: (0, k))] * n
        + [
            pl.BlockSpec((features, STEP_K), lambda k, p, q: (0, k)),
            whole(at_columns),
            whole(down),
        ]
        + [whole(a) for a in before]
        + [pl.BlockSpec(memory_space=pl.ANY)] * len(held),
        out_specs=pl.BlockSpec(memory_space=pl.ANY),
        scratch_shapes=[
            pltpu.VMEM((n * rows, features), jnp.float32),
            pltpu.VMEM((BLOCK, features), jnp.float32),
            pltpu.VMEM((count * rows, features), jnp.bfloat16),
            pltpu.SemaphoreType.DMA((count,)),
        ],
    )
    return pl.pallas_call(
        lambda *refs: frozen_kernel(n, early, first, *refs),
        out_shape=jax.ShapeDtypeStruct((all_rows, features), jnp.bfloat16),
        grid_spec=grid_spec,
        input_output_aliases={n + early + 5: 0} if held else {},
        compiler_params=pltpu.CompilerParams(vmem_limit_bytes=VMEM_BYTES),
        cost_estimate=pl.CostEstimate(
            flops=2 * n * rows * width * features,
            bytes_accessed=2 * width * (features + n * rows),
            transcendentals=0,
        ),
    )(
        places,
        real,
        *shards,
        weight,
        at_columns,
        down,
        *before,
        *held,
    )


def per_device(
    output_cotangent,
    acts,
    output_weight,
    adapter_down_weight,
    adapter_up_weight,
    counts,
    block_tenant_map,
    owner,
):
    f32, bf16 = jnp.float32, jnp.bfloat16
    shard_rows, width = output_cotangent.shape
    features = acts.shape[1]
    held_slots, rank, columns = adapter_up_weight.shape
    nblk_loc = acts.shape[0] // BLOCK
    mp = width // columns
    ring = mp // CORES
    slot_count = owner.shape[0]
    nblocks = block_tenant_map.shape[0]
    group = lax.axis_index("dp")
    member = lax.axis_index("mp")
    z, core = member // CORES, member % CORES
    y, x = group // SIDE, group % SIDE
    at = jnp.stack([x, y, z, core]).astype(jnp.int32)

    def ring_a(v):
        return lax.ppermute(v, "mp", ring_step(1, ring))

    def ring_b(v):
        return lax.ppermute(v, "mp", ring_step(-1, ring))

    def swap(v):
        return lax.ppermute(v, "mp", [(i, i ^ 1) for i in range(mp)])

    same_core = [[r * CORES + c for r in range(ring)] for c in range(CORES)]

    def x_exchange(v):
        return [v] + [lax.ppermute(v, "dp", x_step(shift)) for shift in SHIFTS[1:]]

    def y_exchange(vs):
        moved = zip(SHIFTS[1:], vs[1:])
        return [vs[0]] + [lax.ppermute(v, "dp", y_step(shift)) for shift, v in moved]

    def z_exchange(v):
        return lax.all_to_all(v, "mp", 0, 0, tiled=True, axis_index_groups=same_core)

    toward = 1 - 2 * core

    def places(*steps):
        found = []
        for s in steps:
            chip = (z - s * toward + ring) % ring
            found += [chip * CORES + core, chip * CORES + 1 - core]
        return found

    def shaped(*shape, dtype=bf16):
        return jax.ShapeDtypeStruct(shape, dtype)

    own = output_cotangent
    a1, b1 = ring_a(own), ring_b(own)

    tenant_ids = jnp.arange(slot_count, dtype=jnp.int32)
    global_ids = jnp.arange(nblocks, dtype=jnp.int32)
    slot_blk = jnp.sum(
        jnp.where(block_tenant_map[:, None] == tenant_ids[None, :], owner[None, :], 0), axis=1
    )
    first_block = group * nblk_loc
    local_map = lax.dynamic_slice_in_dim(block_tenant_map, first_block, nblk_loc)
    local_ids = first_block + jnp.arange(nblk_loc, dtype=jnp.int32)
    same = (local_map[:, None] == block_tenant_map[None, :]) & (
        global_ids[None, :] < local_ids[:, None]
    )
    before = jnp.sum(same.astype(jnp.int32), axis=1)
    hit = local_map[:, None] == tenant_ids[None, :]
    limit = jnp.sum(jnp.where(hit, counts[None, :], 0), axis=1)
    real = limit - before * BLOCK

    held = jnp.concatenate([jnp.swapaxes(adapter_down_weight, 1, 2), adapter_up_weight], axis=2)
    near = x_exchange(held)
    picked = local_call(
        pick_kernel,
        [shaped(nblk_loc, rank, features + columns)] * SIDE,
        [at, slot_blk],
        near,
    )
    got = y_exchange(picked)
    mine_cols, other_cols = local_call(
        split_kernel,
        [shaped(shard_rows, width // CORES)] * CORES,
        [at, real],
        [own],
    )
    other_cols = swap(other_cols)
    a2, b2 = ring_a(a1), ring_b(b1)
    down_factor, to_rows = local_call(
        low_kernel,
        [shaped(nblk_loc, rank, features), shaped(nblk_loc, rank, columns + 2 * BLOCK)],
        [],
        [*got, acts],
    )
    at_rows = z_exchange(to_rows)
    early = [early_rows([own, swap(own), a1, swap(b1), b1, swap(a1)], output_weight)]
    a3, b3 = ring_a(a2), ring_b(b2)
    at_rows, early, a2, b2, mine_cols, other_cols = lax.optimization_barrier(
        (at_rows, early, a2, b2, mine_cols, other_cols)
    )
    (sums,) = local_call(
        sums_kernel,
        [shaped(2 * rank, BLOCK, dtype=f32)],
        [at],
        [at_rows, mine_cols, other_cols],
    )
    (to_columns,) = local_call(
        columns_kernel,
        [shaped(ring, rank, columns + BLOCK)],
        [at],
        [sums, swap(sums), mine_cols, other_cols],
    )
    at_columns = z_exchange(to_columns)
    early = early + [early_rows([a2, swap(b2), b2, swap(a2)], output_weight)]
    a4 = ring_a(a3)
    at_columns, early, a3, b3 = lax.optimization_barrier((at_columns, early, a3, b3))
    (grads,) = local_call(
        grads_kernel,
        [shaped(nblk_loc, rank, features + columns)],
        [],
        [at_columns, acts],
    )
    near_grads = x_exchange(grads)
    all_places = jnp.stack(places(0, 1, -1, 2, -2, 3, -3, 4)).astype(jnp.int32)
    out = frozen_rows(
        all_places,
        0,
        7 * CORES,
        real,
        [a3, swap(b3), b3, swap(a3)],
        output_weight,
        at_columns,
        down_factor,
        early,
    )
    near_grads, out, a4 = lax.optimization_barrier((near_grads, out, a4))
    summed = local_call(
        slots_kernel,
        [shaped(held_slots, rank, features + columns)] * SIDE,
        [at, slot_blk],
        near_grads,
        0,
        [pltpu.VMEM((SIDE * held_slots, rank, features + columns), f32)],
    )
    arrived = y_exchange(summed)
    input_gradient = frozen_rows(
        all_places, 7 * CORES, CORES, real, [a4, swap(a4)], output_weight, at_columns, down_factor, (), (out,)
    )
    arrived, input_gradient = lax.optimization_barrier((arrived, input_gradient))
    grad_down, grad_up = local_call(
        finish_kernel,
        [shaped(held_slots, rank, features, dtype=f32), shaped(held_slots, rank, columns, dtype=f32)],
        [],
        arrived,
    )
    return (input_gradient, jnp.swapaxes(grad_down, 1, 2), grad_up)


def solution(mesh):
    in_specs = (
        P(("dp", "mp"), None),
        P("dp", "mp"),
        P("mp", None),
        P("dp", "mp", None),
        P("dp", None, "mp"),
        P(),
        P(),
        P(),
    )
    out_specs = (P("dp", "mp"), P("dp", "mp", None), P("dp", None, "mp"))
    return jax.shard_map(
        per_device, mesh=mesh, in_specs=in_specs, out_specs=out_specs, check_vma=False
    )
```
